256 devices in a mesh: row: 16 (over y, z_hi, core), col: 16 (over x, z_lo).
Axes of the slice: x: 4, y: 4, z: 8 (z_hi: 2, z_lo: 4; z = z_hi * 4 + z_lo), core: 2. Of those that a mesh axis runs over, the one named last changes fastest.
Arguments:
- images: bfloat16 [196608, 1152], P(('row', 'col')), may hold values from -6 to 6
- texts: bfloat16 [196608, 1152], P(('row', 'col')), may hold values from -6 to 6
- logit_scale: float32 [1], replicated, may hold values from 0.01 to 0.03
- logit_bias: float32 [1], replicated, may hold values from -2 to -0.5
Outputs:
- image_grad: bfloat16 [196608, 1152], P(('row', 'col'))
- text_grad: bfloat16 [196608, 1152], P(('row', 'col'))
The draws below stay inside these ranges and needn't reach their ends.
All inputs are finite; a program needn't handle non-finite values.
Results may differ from the reference program's by a relative error of at most 0.0042.
Values may be sent and summed in bfloat16 or wider, within the bound.
A program may use at most 64 MiB of HBM per device.

```python
import math
import jax
import jax.numpy as jnp
from jax import lax

D = 1152
B_DEV = 768
BATCH = 196608
N_ROW = 16
N_COL = 16


def block_levels(stream_key, shape, split, low, top_value):
    def one(position, shards_of):
        steps = jax.random.uniform(jax.random.fold_in(jax.random.fold_in(stream_key, 6), position), (shards_of,), jnp.float32, low / len(split), top_value / len(split))
        return jnp.repeat(jnp.exp(steps), shape[position] // shards_of).reshape((-1,) + (1,) * (len(shape) - position - 1))

    gain = one(*split[0])
    for cut in split[1:]:
        gain = gain * one(*cut)
    return gain


def centred(rng, extent, spread, most, split=(), kind=jnp.bfloat16):
    entries = jax.random.normal(rng, extent, jnp.float32) * spread
    if len(split) > 0:
        entries = block_levels(rng, extent, split, -0.22, 0.18) * entries
    return jnp.clip(entries, min=-most, max=most).astype(kind)


def setup_inputs(seed: int = 0) -> dict:
    splits = jax.random.split(jax.random.key(seed), 5)
    return {
        "images": centred(splits[0], (BATCH, D), 1.0, 6.0, ((0, 256),)),
        "texts": centred(splits[1], (BATCH, D), 1.0, 6.0, ((0, 256),)),
        "logit_scale": jnp.clip(jnp.exp(jax.random.uniform(splits[2], (1,), jnp.float32, math.log(0.01), math.log(0.03))), 0.01, 0.03),
        "logit_bias": jnp.clip(jax.random.uniform(splits[3], (1,), jnp.float32, -2.0, -0.5), -2.0, -0.5),
    }


def block_grad(left, right, scale, bias, positive):
    logits = jnp.dot(left, right.T, preferred_element_type=jnp.float32) * scale + bias
    eye_mask = jnp.eye(left.shape[0], dtype=jnp.float32) * positive
    return (jax.nn.sigmoid(logits) - eye_mask).astype(jnp.bfloat16)

def reference(images, texts, logit_scale, logit_bias):
    count = N_ROW * N_COL
    scale = logit_scale[0]
    bias = logit_bias[0]
    image_blocks = images.reshape(count, B_DEV, D)
    text_blocks = texts.reshape(count, B_DEV, D)
    first_mask = N_ROW // 2 * N_COL
    second_mask = N_COL // 2

    def visit(text_acc, index):
        left = lax.dynamic_index_in_dim(image_blocks, index, 0, keepdims=False)
        image_acc = jnp.zeros((B_DEV, D), jnp.float32)
        partners = (index, jnp.bitwise_xor(index, first_mask).astype(jnp.int32), jnp.bitwise_xor(index, second_mask).astype(jnp.int32))
        for number in range(3):
            other = partners[number]
            right = lax.dynamic_index_in_dim(text_blocks, other, 0, keepdims=False)
            grad = block_grad(left, right, scale, bias, 1.0 if number == 0 else 0.0)
            image_acc = image_acc + scale * jnp.dot(grad, right, preferred_element_type=jnp.float32)
            text_part = scale * jnp.dot(grad.T, left, preferred_element_type=jnp.float32)
            text_acc = text_acc.at[other].add(text_part)
        return (text_acc, image_acc)
    text_init = jnp.zeros((count, B_DEV, D), jnp.float32)
    text_acc, image_acc = lax.scan(visit, text_init, jnp.arange(count, dtype=jnp.int32))
    image_grad = image_acc.reshape(count * B_DEV, D).astype(jnp.bfloat16)
    text_grad = text_acc.reshape(count * B_DEV, D).astype(jnp.bfloat16)
    return (image_grad, text_grad)
```

```python
import functools

import jax
import jax.numpy as jnp
from jax import lax
from jax.experimental import pallas as pl
from jax.experimental.pallas import tpu as pltpu
from jax.sharding import PartitionSpec as P

MESH = pl.DeviceIdType.MESH
CHUNK = 128
TAIL = (64, 32, 32)
AHEAD = 3
TILE = 256


def products(left, block, scale, bias, accumulate, diagonal=None):
    height, width = left.shape[0], block.shape[0]

    def tile(index, _):
        rows = pl.ds(pl.multiple_of(index * TILE, TILE), TILE)
        logits = lax.dot_general(
            left[rows, :], block[...], (((1,), (1,)), ((), ())), preferred_element_type=jnp.float32
        )
        value = jax.nn.sigmoid(logits * scale + bias)
        if diagonal is not None:
            here = lax.broadcasted_iota(jnp.int32, (TILE, width), 0) + index * TILE
            there = lax.broadcasted_iota(jnp.int32, (TILE, width), 1) + diagonal
            value = value - jnp.where(here == there, 1.0, 0.0)
        accumulate(rows, value.astype(jnp.bfloat16))
        return 0

    lax.fori_loop(0, height // TILE, tile, 0)


def exchange_kernel(
    images, texts, scale_ref, bias_ref, acc, image_out, last_grad, last_block, scale_out,
    own, got, send_sem, recv_sem, load_sem,
):
    rows = images.shape[0]
    row, col = lax.axis_index("row"), lax.axis_index("col")
    n_row, n_col = lax.axis_size("row"), lax.axis_size("col")
    partners = (
        (row, lax.rem(col + n_col // 2, n_col)),
        (lax.rem(row + n_row // 2, n_row), col),
    )
    per_unit = rows // CHUNK
    whole = 2 * per_unit - sum(TAIL) // CHUNK
    tail_at = [rows - sum(TAIL[j:]) for j in range(len(TAIL))]
    sources = (texts, images)

    barrier = pltpu.get_barrier_semaphore()
    for partner in partners:
        pl.semaphore_signal(barrier, inc=1, device_id=partner, device_id_type=MESH)
    pl.semaphore_wait(barrier, len(partners))

    def copies(unit, start, size, step):
        found = []
        for axis, partner in enumerate(partners):
            place = 2 * start + axis * size
            if not isinstance(place, int):
                place = pl.multiple_of(place, CHUNK)
            target = (
                last_block.at[pl.ds(axis * size, size)]
                if isinstance(step, int) and step == whole + len(TAIL) - 1
                else got.at[unit, pl.ds(place, size)]
            )
            found.append(
                pltpu.make_async_remote_copy(
                    src_ref=sources[unit].at[pl.ds(start, size)],
                    dst_ref=target,
                    send_sem=send_sem.at[axis, step],
                    recv_sem=recv_sem.at[axis, step],
                    device_id=partner,
                    device_id_type=MESH,
                )
            )
        return found

    def tail_copies(j):
        return copies(1, tail_at[j], TAIL[j], whole + j)

    def start_step(step):
        if isinstance(step, int):
            if step < whole:
                found = copies(step // per_unit, step % per_unit * CHUNK, CHUNK, step)
            else:
                found = tail_copies(step - whole)
            for copy in found:
                copy.start()
            return
        for unit in range(2):
            low, high = unit * per_unit, min((unit + 1) * per_unit, whole)

            @pl.when((step >= low) & (step < high))
            def _():
                start = pl.multiple_of((step - low) * CHUNK, CHUNK)
                for copy in copies(unit, start, CHUNK, step):
                    copy.start()

        for j in range(len(TAIL)):

            @pl.when(step == whole + j)
            def _():
                start_step(whole + j)

    for step in range(AHEAD):
        start_step(step)

    loads = [
        pltpu.make_async_copy(images, own.at[0], load_sem.at[0]),
        pltpu.make_async_copy(texts, own.at[1], load_sem.at[1]),
    ]
    for load in loads:
        load.start()
    for load in loads:
        load.wait()
    scale, bias = scale_ref[0], bias_ref[0]
    scale_out[...] = jnp.full(scale_out.shape, scale, jnp.float32)

    def add_to(unit, block):
        def accumulate(tile_rows, grad):
            acc[unit, tile_rows, :] += jnp.dot(
                grad, block[...], preferred_element_type=jnp.float32
            )

        return accumulate

    for unit in range(2):
        acc[unit] = jnp.zeros((rows, acc.shape[2]), jnp.float32)

        def own_block(index, _):
            at = pl.multiple_of(index * TILE, TILE)
            block = own.at[1 - unit, pl.ds(at, TILE)]
            products(own.at[unit], block, scale, bias, add_to(unit, block), diagonal=at)
            return 0

        lax.fori_loop(0, rows // TILE, own_block, 0)

    def wait_step(unit, start, size, step):
        for copy in copies(unit, start, size, step):
            copy.wait()

    for unit in range(2):
        low, high = unit * per_unit, min((unit + 1) * per_unit, whole)

        def met_block(step, _):
            start = pl.multiple_of((step - low) * CHUNK, CHUNK)
            wait_step(unit, start, CHUNK, step)
            start_step(step + AHEAD)
            block = got.at[unit, pl.ds(pl.multiple_of(2 * start, 2 * CHUNK), 2 * CHUNK)]
            products(own.at[unit], block, scale, bias, add_to(unit, block))
            return 0

        lax.fori_loop(low, high, met_block, 0)
        if unit == 0:
            image_out[...] = (acc[0] * scale).astype(jnp.bfloat16)

    for j in range(len(TAIL)):
        wait_step(1, tail_at[j], TAIL[j], whole + j)
        if whole + j + AHEAD < whole + len(TAIL):
            start_step(whole + j + AHEAD)
        if j < len(TAIL) - 1:
            block = got.at[1, pl.ds(2 * tail_at[j], 2 * TAIL[j])]
            products(own.at[1], block, scale, bias, add_to(1, block))
        else:

            def keep(tile_rows, grad):
                last_grad[tile_rows, :] = grad

            products(own.at[1], last_block, scale, bias, keep)


def finish_kernel(acc, image_in, last_grad, last_block, scale_in, image_out, text_out, text, sem):
    rows = text.shape[0]
    image_copy = pltpu.make_async_copy(image_in, image_out, sem.at[0])
    image_copy.start()
    scale = scale_in[0:1, 0:1]
    text_copies = []
    for index in range(rows // TILE):
        tile_rows = pl.ds(index * TILE, TILE)
        total = acc[1, tile_rows, :] + jnp.dot(
            last_grad[tile_rows, :], last_block[...], preferred_element_type=jnp.float32
        )
        text[tile_rows, :] = (total * scale).astype(jnp.bfloat16)
        copy = pltpu.make_async_copy(
            text.at[tile_rows], text_out.at[tile_rows], sem.at[1 + index]
        )
        copy.start()
        text_copies.append(copy)
    image_copy.wait()
    for copy in text_copies:
        copy.wait()


def shards(images, texts, logit_scale, logit_bias):
    rows, width = images.shape
    steps = 2 * (rows // CHUNK) - sum(TAIL) // CHUNK + len(TAIL)
    hbm = pl.BlockSpec(memory_space=pltpu.HBM)
    vmem = pl.BlockSpec(memory_space=pltpu.VMEM)
    smem = pl.BlockSpec(memory_space=pltpu.SMEM)
    kept = pl.pallas_call(
        exchange_kernel,
        out_shape=[
            pltpu.VMEM((2, rows, width), jnp.float32),
            pltpu.VMEM((rows, width), jnp.bfloat16),
            pltpu.VMEM((rows, 2 * TAIL[-1]), jnp.bfloat16),
            pltpu.VMEM((2 * TAIL[-1], width), jnp.bfloat16),
            pltpu.VMEM((8, 128), jnp.float32),
        ],
        in_specs=[hbm, hbm, smem, smem],
        out_specs=[vmem] * 5,
        scratch_shapes=[
            pltpu.VMEM((2, rows, width), jnp.bfloat16),
            pltpu.VMEM((2, 2 * rows, width), jnp.bfloat16),
            pltpu.SemaphoreType.DMA((2, steps)),
            pltpu.SemaphoreType.DMA((2, steps)),
            pltpu.SemaphoreType.DMA((2,)),
        ],
        compiler_params=pltpu.CompilerParams(
            collective_id=0, has_side_effects=True, vmem_limit_bytes=32 << 20
        ),
        name="exchange",
    )(
        pltpu.with_memory_space_constraint(images, pltpu.HBM),
        pltpu.with_memory_space_constraint(texts, pltpu.HBM),
        logit_scale,
        logit_bias,
    )
    kept = [pltpu.with_memory_space_constraint(x, pltpu.VMEM) for x in kept]
    return pl.pallas_call(
        finish_kernel,
        out_shape=[jax.ShapeDtypeStruct((rows, width), jnp.bfloat16)] * 2,
        in_specs=[vmem] * 5,
        out_specs=[hbm] * 2,
        scratch_shapes=[
            pltpu.VMEM((rows, width), jnp.bfloat16),
            pltpu.SemaphoreType.DMA((1 + rows // TILE,)),
        ],
        compiler_params=pltpu.CompilerParams(vmem_limit_bytes=16 << 20),
        name="finish",
    )(*kept)


def solution(mesh):
    placed = (P(("row", "col"), None), P(("row", "col"), None), P(), P())
    return jax.shard_map(
        shards,
        mesh=mesh,
        in_specs=placed,
        out_specs=(P(("row", "col"), None), P(("row", "col"), None)),
        check_vma=False,
    )
```

```python
import jax
import jax.numpy as jnp
from jax import lax
from jax.experimental import pallas as pl
from jax.experimental.pallas import tpu as pltpu
from jax.sharding import PartitionSpec as P

MESH = pl.DeviceIdType.MESH
CHUNK = 128
FIRST = 2
BLOCK = 2 * CHUNK


def gradient(left, block, scale, bias, diagonal=None):
    logits = lax.dot_general(
        left[...], block[...], (((1,), (1,)), ((), ())), preferred_element_type=jnp.float32
    )
    value = jax.nn.sigmoid(logits * scale + bias)
    if diagonal is not None:
        here = lax.broadcasted_iota(jnp.int32, value.shape, 0)
        there = lax.broadcasted_iota(jnp.int32, value.shape, 1) + diagonal
        value = value - jnp.where(here == there, 1.0, 0.0)
    return value.astype(jnp.bfloat16)


def exchange_kernel(
    images, texts, scale_ref, bias_ref, acc, image_out, last_grad, got, scale_out,
    own, send_sem, recv_sem, load_sem, ready,
):
    rows = images.shape[0]
    row, col = lax.axis_index("row"), lax.axis_index("col")
    n_row, n_col = lax.axis_size("row"), lax.axis_size("col")
    partners = (
        (row, lax.rem(col + n_col // 2, n_col)),
        (lax.rem(row + n_row // 2, n_row), col),
    )
    per_unit = rows // CHUNK
    steps = 2 * per_unit
    sources = (texts, images)

    def transfer(axis, unit, index):
        step = unit * per_unit + index
        start = index * CHUNK
        if not isinstance(start, int):
            start = pl.multiple_of(start, CHUNK)
        return pltpu.make_async_remote_copy(
            src_ref=sources[unit].at[pl.ds(start, CHUNK)],
            dst_ref=got.at[step, pl.ds(axis * CHUNK, CHUNK)],
            send_sem=send_sem.at[axis, step],
            recv_sem=recv_sem.at[axis, step],
            device_id=partners[axis],
            device_id_type=MESH,
        )

    halves = (col >= n_col // 2, row >= n_row // 2)
    barrier = pltpu.get_barrier_semaphore()
    for axis in range(2):

        @pl.when(jnp.logical_not(halves[axis]))
        def _():
            pl.semaphore_signal(barrier, inc=1, device_id=partners[axis], device_id_type=MESH)

    @pl.when(jnp.logical_or(halves[0], halves[1]))
    def _():
        pl.semaphore_wait(barrier, halves[0].astype(jnp.int32) + halves[1].astype(jnp.int32))

    for axis in range(2):

        @pl.when(halves[axis])
        def _():
            pl.semaphore_signal(
                ready.at[axis], inc=1, device_id=partners[axis], device_id_type=MESH
            )
            for step in range(FIRST):
                transfer(axis, step // per_unit, step % per_unit).start()

    for axis in range(2):

        @pl.when(jnp.logical_not(halves[axis]))
        def _():
            pl.semaphore_wait(ready.at[axis], 1)
            for step in range(FIRST):
                transfer(axis, step // per_unit, step % per_unit).start()

    for step in range(FIRST, steps):
        for axis in range(2):
            transfer(axis, step // per_unit, step % per_unit).start()

    loads = [
        pltpu.make_async_copy(images, own.at[0], load_sem.at[0]),
        pltpu.make_async_copy(texts, own.at[1], load_sem.at[1]),
    ]
    for load in loads:
        load.start()
    for load in loads:
        load.wait()
    scale, bias = scale_ref[0], bias_ref[0]
    scale_out[...] = jnp.full(scale_out.shape, scale, jnp.float32)

    for unit in range(2):

        def own_block(index, _):
            at = pl.multiple_of(index * BLOCK, BLOCK)
            block = own.at[1 - unit, pl.ds(at, BLOCK)]
            grad = gradient(own.at[unit], block, scale, bias, at)
            acc[unit] += jnp.dot(grad, block[...], preferred_element_type=jnp.float32)
            return 0

        acc[unit] = jnp.zeros(acc.shape[1:], jnp.float32)
        lax.fori_loop(0, rows // BLOCK, own_block, 0)

    for unit in range(2):

        def met_block(index, _):
            step = unit * per_unit + index
            for axis in range(2):
                transfer(axis, unit, index).wait()
            block = got.at[step]
            grad = gradient(own.at[unit], block, scale, bias)
            if unit == 0:
                acc[unit] += jnp.dot(grad, block[...], preferred_element_type=jnp.float32)
            else:
                last_grad[...] = grad

                @pl.when(step < steps - 1)
                def _():
                    acc[unit] += jnp.dot(grad, block[...], preferred_element_type=jnp.float32)

            return 0

        lax.fori_loop(0, per_unit, met_block, 0)
        if unit == 0:
            image_out[...] = (acc[0] * scale).astype(jnp.bfloat16)


def finish_kernel(acc, image_in, last_grad, got, scale_in, image_out, text_out, text, sem):
    rows = text.shape[0]
    image_copy = pltpu.make_async_copy(image_in, image_out, sem.at[0])
    image_copy.start()
    scale = scale_in[0:1, 0:1]
    last = got.shape[0] - 1
    text_copies = []
    for index in range(rows // BLOCK):
        part = pl.ds(index * BLOCK, BLOCK)
        total = acc[1, part, :] + jnp.dot(
            last_grad[part, :], got[last], preferred_element_type=jnp.float32
        )
        text[part, :] = (total * scale).astype(jnp.bfloat16)
        copy = pltpu.make_async_copy(text.at[part], text_out.at[part], sem.at[1 + index])
        copy.start()
        text_copies.append(copy)
    image_copy.wait()
    for copy in text_copies:
        copy.wait()


def shards(images, texts, logit_scale, logit_bias):
    rows, width = images.shape
    steps = 2 * (rows // CHUNK)
    hbm = pl.BlockSpec(memory_space=pltpu.HBM)
    vmem = pl.BlockSpec(memory_space=pltpu.VMEM)
    smem = pl.BlockSpec(memory_space=pltpu.SMEM)
    kept = pl.pallas_call(
        exchange_kernel,
        out_shape=[
            pltpu.VMEM((2, rows, width), jnp.float32),
            pltpu.VMEM((rows, width), jnp.bfloat16),
            pltpu.VMEM((rows, BLOCK), jnp.bfloat16),
            pltpu.VMEM((steps, BLOCK, width), jnp.bfloat16),
            pltpu.VMEM((8, 128), jnp.float32),
        ],
        in_specs=[hbm, hbm, smem, smem],
        out_specs=[vmem] * 5,
        scratch_shapes=[
            pltpu.VMEM((2, rows, width), jnp.bfloat16),
            pltpu.SemaphoreType.DMA((2, steps)),
            pltpu.SemaphoreType.DMA((2, steps)),
            pltpu.SemaphoreType.DMA((2,)),
            pltpu.SemaphoreType.REGULAR((2,)),
        ],
        compiler_params=pltpu.CompilerParams(
            collective_id=0, has_side_effects=True, vmem_limit_bytes=32 << 20
        ),
        name="exchange",
    )(
        pltpu.with_memory_space_constraint(images, pltpu.HBM),
        pltpu.with_memory_space_constraint(texts, pltpu.HBM),
        logit_scale,
        logit_bias,
    )
    kept = [pltpu.with_memory_space_constraint(x, pltpu.VMEM) for x in kept]
    return pl.pallas_call(
        finish_kernel,
        out_shape=[jax.ShapeDtypeStruct((rows, width), jnp.bfloat16)] * 2,
        in_specs=[vmem] * 5,
        out_specs=[hbm] * 2,
        scratch_shapes=[
            pltpu.VMEM((rows, width), jnp.bfloat16),
            pltpu.SemaphoreType.DMA((1 + rows // BLOCK,)),
        ],
        compiler_params=pltpu.CompilerParams(vmem_limit_bytes=16 << 20),
        name="finish",
    )(*kept)


def solution(mesh):
    placed = (P(("row", "col"), None), P(("row", "col"), None), P(), P())
    return jax.shard_map(
        shards,
        mesh=mesh,
        in_specs=placed,
        out_specs=(P(("row", "col"), None), P(("row", "col"), None)),
        check_vma=False,
    )
```

```python
import jax
import jax.numpy as jnp
from jax import lax
from jax.experimental import pallas as pl
from jax.experimental.pallas import tpu as pltpu
from jax.sharding import PartitionSpec as P

MESH = pl.DeviceIdType.MESH
CHUNKS = ((384, 384), (384, 256, 128))
BLOCK = 256
LAST = 1024


def gradient(left, block, scale, bias, diagonal=None):
    logits = lax.dot_general(
        left[...], block[...], (((1,), (1,)), ((), ())), preferred_element_type=jnp.float32
    )
    value = jax.nn.sigmoid(logits * scale + bias)
    if diagonal is not None:
        here = lax.broadcasted_iota(jnp.int32, value.shape, 0)
        there = lax.broadcasted_iota(jnp.int32, value.shape, 1) + diagonal
        value = value - jnp.where(here == there, 1.0, 0.0)
    return value.astype(jnp.bfloat16)


def exchange_kernel(
    images, texts, scale_ref, bias_ref, acc, image_out, last_grad, got, scale_out,
    own, logits, send_sem, recv_sem, load_sem, ready,
):
    rows = images.shape[0]
    row, col = lax.axis_index("row"), lax.axis_index("col")
    n_row, n_col = lax.axis_size("row"), lax.axis_size("col")
    partners = (
        (row, lax.rem(col + n_col // 2, n_col)),
        (lax.rem(row + n_row // 2, n_row), col),
    )
    per_unit = 2 * rows // BLOCK
    plan = []
    for unit, sizes in enumerate(CHUNKS):
        start = 0
        for size in sizes:
            plan.append((unit, start, size, 0, images.shape[1]))
            start += size
    unit, start, size, _, width = plan.pop()
    plan += [(unit, start, size, 0, LAST), (unit, start, size, LAST, width - LAST)]
    sources = (texts, images)

    def transfer(axis, number):
        unit, start, size, left, width = plan[number]
        columns = pl.ds(left, width)
        place = 2 * (unit * rows + start) + axis * size
        return pltpu.make_async_remote_copy(
            src_ref=sources[unit].at[pl.ds(start, size), columns],
            dst_ref=got.at[pl.ds(place, size), columns],
            send_sem=send_sem.at[axis, number],
            recv_sem=recv_sem.at[axis, number],
            device_id=partners[axis],
            device_id_type=MESH,
        )

    halves = (col >= n_col // 2, row >= n_row // 2)
    barrier = pltpu.get_barrier_semaphore()
    for axis in range(2):

        @pl.when(jnp.logical_not(halves[axis]))
        def _():
            pl.semaphore_signal(barrier, inc=1, device_id=partners[axis], device_id_type=MESH)

    @pl.when(jnp.logical_or(halves[0], halves[1]))
    def _():
        pl.semaphore_wait(barrier, halves[0].astype(jnp.int32) + halves[1].astype(jnp.int32))

    for axis in range(2):

        @pl.when(halves[axis])
        def _():
            pl.semaphore_signal(
                ready.at[axis], inc=1, device_id=partners[axis], device_id_type=MESH
            )
            transfer(axis, 0).start()

    for axis in range(2):

        @pl.when(jnp.logical_not(halves[axis]))
        def _():
            pl.semaphore_wait(ready.at[axis], 1)
            transfer(axis, 0).start()

    for number in range(1, len(plan)):
        for axis in range(2):
            transfer(axis, number).start()

    loads = [
        pltpu.make_async_copy(images, own.at[0], load_sem.at[0]),
        pltpu.make_async_copy(texts, own.at[1], load_sem.at[1]),
    ]
    for load in loads:
        load.start()
    for load in loads:
        load.wait()
    scale, bias = scale_ref[0], bias_ref[0]
    scale_out[...] = jnp.full(scale_out.shape, scale, jnp.float32)

    for unit in range(2):

        def own_block(index, _):
            at = pl.multiple_of(index * BLOCK, BLOCK)
            block = own.at[1 - unit, pl.ds(at, BLOCK)]
            grad = gradient(own.at[unit], block, scale, bias, at)
            acc[unit] += jnp.dot(grad, block[...], preferred_element_type=jnp.float32)
            return 0

        acc[unit] = jnp.zeros(acc.shape[1:], jnp.float32)
        lax.fori_loop(0, rows // BLOCK, own_block, 0)

    for unit in range(2):
        blocks = per_unit - unit

        def met_block(index, _):
            for number, (owner, start, *_rest) in enumerate(plan[:-2]):
                if owner == unit:

                    @pl.when(index == 2 * start // BLOCK)
                    def _():
                        for axis in range(2):
                            transfer(axis, number).wait()

            at = pl.multiple_of((unit * per_unit + index) * BLOCK, BLOCK)
            block = got.at[pl.ds(at, BLOCK)]
            grad = gradient(own.at[unit], block, scale, bias)
            acc[unit] += jnp.dot(grad, block[...], preferred_element_type=jnp.float32)
            return 0

        lax.fori_loop(0, blocks, met_block, 0)
        if unit == 0:
            image_out[...] = (acc[0] * scale).astype(jnp.bfloat16)

    last = pl.ds(got.shape[0] - BLOCK, BLOCK)
    for number, columns in ((-2, pl.ds(0, LAST)), (-1, pl.ds(LAST, images.shape[1] - LAST))):
        for axis in range(2):
            transfer(axis, len(plan) + number).wait()
        part = lax.dot_general(
            own[1, :, columns], got[last, columns], (((1,), (1,)), ((), ())),
            preferred_element_type=jnp.float32,
        )
        if number == -2:
            logits[...] = part
        else:
            value = jax.nn.sigmoid((logits[...] + part) * scale + bias)
            last_grad[...] = value.astype(jnp.bfloat16)


def finish_kernel(acc, image_in, last_grad, got, scale_in, image_out, text_out, text, sem):
    rows = text.shape[0]
    image_copy = pltpu.make_async_copy(image_in, image_out, sem.at[0])
    image_copy.start()
    scale = scale_in[0:1, 0:1]
    last = got.shape[0] - BLOCK
    text_copies = []
    for index in range(rows // BLOCK):
        part = pl.ds(index * BLOCK, BLOCK)
        total = acc[1, part, :] + jnp.dot(
            last_grad[part, :], got[pl.ds(last, BLOCK)], preferred_element_type=jnp.float32
        )
        text[part, :] = (total * scale).astype(jnp.bfloat16)
        copy = pltpu.make_async_copy(text.at[part], text_out.at[part], sem.at[1 + index])
        copy.start()
        text_copies.append(copy)
    image_copy.wait()
    for copy in text_copies:
        copy.wait()


def shards(images, texts, logit_scale, logit_bias):
    rows, width = images.shape
    chunks = sum(len(sizes) for sizes in CHUNKS) + 1
    hbm = pl.BlockSpec(memory_space=pltpu.HBM)
    vmem = pl.BlockSpec(memory_space=pltpu.VMEM)
    smem = pl.BlockSpec(memory_space=pltpu.SMEM)
    kept = pl.pallas_call(
        exchange_kernel,
        out_shape=[
            pltpu.VMEM((2, rows, width), jnp.float32),
            pltpu.VMEM((rows, width), jnp.bfloat16),
            pltpu.VMEM((rows, BLOCK), jnp.bfloat16),
            pltpu.VMEM((4 * rows, width), jnp.bfloat16),
            pltpu.VMEM((8, 128), jnp.float32),
        ],
        in_specs=[hbm, hbm, smem, smem],
        out_specs=[vmem] * 5,
        scratch_shapes=[
            pltpu.VMEM((2, rows, width), jnp.bfloat16),
            pltpu.VMEM((rows, BLOCK), jnp.float32),
            pltpu.SemaphoreType.DMA((2, chunks)),
            pltpu.SemaphoreType.DMA((2, chunks)),
            pltpu.SemaphoreType.DMA((2,)),
            pltpu.SemaphoreType.REGULAR((2,)),
        ],
        compiler_params=pltpu.CompilerParams(
            collective_id=0, has_side_effects=True, vmem_limit_bytes=32 << 20
        ),
        name="exchange",
    )(
        pltpu.with_memory_space_constraint(images, pltpu.HBM),
        pltpu.with_memory_space_constraint(texts, pltpu.HBM),
        logit_scale,
        logit_bias,
    )
    kept = [pltpu.with_memory_space_constraint(x, pltpu.VMEM) for x in kept]
    return pl.pallas_call(
        finish_kernel,
        out_shape=[jax.ShapeDtypeStruct((rows, width), jnp.bfloat16)] * 2,
        in_specs=[vmem] * 5,
        out_specs=[hbm] * 2,
        scratch_shapes=[
            pltpu.VMEM((rows, width), jnp.bfloat16),
            pltpu.SemaphoreType.DMA((1 + rows // BLOCK,)),
        ],
        compiler_params=pltpu.CompilerParams(vmem_limit_bytes=16 << 20),
        name="finish",
    )(*kept)


def solution(mesh):
    placed = (P(("row", "col"), None), P(("row", "col"), None), P(), P())
    return jax.shard_map(
        shards,
        mesh=mesh,
        in_specs=placed,
        out_specs=(P(("row", "col"), None), P(("row", "col"), None)),
        check_vma=False,
    )
```

```python
import jax
import jax.numpy as jnp
from jax import lax
from jax.experimental import pallas as pl
from jax.experimental.pallas import tpu as pltpu
from jax.sharding import PartitionSpec as P

MESH = pl.DeviceIdType.MESH
CHUNKS = ((384, 384), (384, 256, 128))
BLOCK = 256
LAST = 1024


def gradient(left, block, scale, bias, diagonal=None):
    logits = lax.dot_general(
        left[...], block[...], (((1,), (1,)), ((), ())), preferred_element_type=jnp.float32
    )
    value = jax.nn.sigmoid(logits * scale + bias)
    if diagonal is not None:
        here = lax.broadcasted_iota(jnp.int32, value.shape, 0)
        there = lax.broadcasted_iota(jnp.int32, value.shape, 1) + diagonal
        value = value - jnp.where(here == there, 1.0, 0.0)
    return value.astype(jnp.bfloat16)


def exchange_kernel(
    images, texts, scale_ref, bias_ref, acc, image_out, last_grad, got, scale_out,
    own, logits, send_sem, recv_sem, load_sem, ready,
):
    rows = images.shape[0]
    row, col = lax.axis_index("row"), lax.axis_index("col")
    n_row, n_col = lax.axis_size("row"), lax.axis_size("col")
    partners = (
        (row, lax.rem(col + n_col // 2, n_col)),
        (lax.rem(row + n_row // 2, n_row), col),
    )
    per_unit = 2 * rows // BLOCK
    plan = []
    for unit, sizes in enumerate(CHUNKS):
        start = 0
        for size in sizes:
            plan.append((unit, start, size, 0, images.shape[1]))
            start += size
    unit, start, size, _, width = plan.pop()
    plan += [(unit, start, size, 0, LAST), (unit, start, size, LAST, width - LAST)]
    sources = (texts, images)

    def transfer(axis, number):
        unit, start, size, left, width = plan[number]
        columns = pl.ds(left, width)
        place = 2 * (unit * rows + start) + axis * size
        return pltpu.make_async_remote_copy(
            src_ref=sources[unit].at[pl.ds(start, size), columns],
            dst_ref=got.at[pl.ds(place, size), columns],
            send_sem=send_sem.at[axis, number],
            recv_sem=recv_sem.at[axis, number],
            device_id=partners[axis],
            device_id_type=MESH,
        )

    halves = (col >= n_col // 2, row >= n_row // 2)
    lower = (jnp.logical_not(halves[0]), jnp.logical_not(halves[1]))
    greeting = ((lower[0] | lower[1]), lower[1])
    greeted = ((halves[0] | lower[1]), halves[1])
    barrier = pltpu.get_barrier_semaphore()
    for axis in range(2):

        @pl.when(greeting[axis])
        def _():
            pl.semaphore_signal(barrier, inc=1, device_id=partners[axis], device_id_type=MESH)

    pl.semaphore_wait(barrier, greeted[0].astype(jnp.int32) + greeted[1].astype(jnp.int32))

    for axis in range(2):

        @pl.when(jnp.logical_not(greeting[axis]))
        def _():
            pl.semaphore_signal(
                ready.at[axis], inc=1, device_id=partners[axis], device_id_type=MESH
            )

    for axis in range(2):

        @pl.when(greeted[axis])
        def _():
            transfer(axis, 0).start()

    for axis in range(2):

        @pl.when(jnp.logical_not(greeted[axis]))
        def _():
            pl.semaphore_wait(ready.at[axis], 1)
            transfer(axis, 0).start()

    for number in range(1, len(plan)):
        for axis in range(2):
            transfer(axis, number).start()

    loads = [
        pltpu.make_async_copy(images, own.at[0], load_sem.at[0]),
        pltpu.make_async_copy(texts, own.at[1], load_sem.at[1]),
    ]
    for load in loads:
        load.start()
    for load in loads:
        load.wait()
    scale, bias = scale_ref[0], bias_ref[0]
    scale_out[...] = jnp.full(scale_out.shape, scale, jnp.float32)

    for unit in range(2):

        def own_block(index, _):
            at = pl.multiple_of(index * BLOCK, BLOCK)
            block = own.at[1 - unit, pl.ds(at, BLOCK)]
            grad = gradient(own.at[unit], block, scale, bias, at)
            acc[unit] += jnp.dot(grad, block[...], preferred_element_type=jnp.float32)
            return 0

        acc[unit] = jnp.zeros(acc.shape[1:], jnp.float32)
        lax.fori_loop(0, rows // BLOCK, own_block, 0)

    for unit in range(2):
        blocks = per_unit - unit

        def met_block(index, _):
            for number, (owner, start, *_rest) in enumerate(plan[:-2]):
                if owner == unit:

                    @pl.when(index == 2 * start // BLOCK)
                    def _():
                        for axis in range(2):
                            transfer(axis, number).wait_recv()

            at = pl.multiple_of((unit * per_unit + index) * BLOCK, BLOCK)
            block = got.at[pl.ds(at, BLOCK)]
            grad = gradient(own.at[unit], block, scale, bias)
            acc[unit] += jnp.dot(grad, block[...], preferred_element_type=jnp.float32)
            return 0

        lax.fori_loop(0, blocks, met_block, 0)
        if unit == 0:
            image_out[...] = (acc[0] * scale).astype(jnp.bfloat16)

    last = pl.ds(got.shape[0] - BLOCK, BLOCK)
    for number, columns in ((-2, pl.ds(0, LAST)), (-1, pl.ds(LAST, images.shape[1] - LAST))):
        for axis in range(2):
            transfer(axis, len(plan) + number).wait_recv()
        part = lax.dot_general(
            own[1, :, columns], got[last, columns], (((1,), (1,)), ((), ())),
            preferred_element_type=jnp.float32,
        )
        if number == -2:
            logits[...] = part
        else:
            value = jax.nn.sigmoid((logits[...] + part) * scale + bias)
            last_grad[...] = value.astype(jnp.bfloat16)

    for number in range(len(plan)):
        for axis in range(2):
            transfer(axis, number).wait_send()


def finish_kernel(acc, image_in, last_grad, got, scale_in, image_out, text_out, text, sem):
    rows = text.shape[0]
    image_copy = pltpu.make_async_copy(image_in, image_out, sem.at[0])
    image_copy.start()
    scale = scale_in[0:1, 0:1]
    last = got.shape[0] - BLOCK
    text_copies = []
    for index in range(rows // BLOCK):
        part = pl.ds(index * BLOCK, BLOCK)
        total = acc[1, part, :] + jnp.dot(
            last_grad[part, :], got[pl.ds(last, BLOCK)], preferred_element_type=jnp.float32
        )
        text[part, :] = (total * scale).astype(jnp.bfloat16)
        copy = pltpu.make_async_copy(text.at[part], text_out.at[part], sem.at[1 + index])
        copy.start()
        text_copies.append(copy)
    image_copy.wait()
    for copy in text_copies:
        copy.wait()


def shards(images, texts, logit_scale, logit_bias):
    rows, width = images.shape
    chunks = sum(len(sizes) for sizes in CHUNKS) + 1
    hbm = pl.BlockSpec(memory_space=pltpu.HBM)
    vmem = pl.BlockSpec(memory_space=pltpu.VMEM)
    smem = pl.BlockSpec(memory_space=pltpu.SMEM)
    kept = pl.pallas_call(
        exchange_kernel,
        out_shape=[
            pltpu.VMEM((2, rows, width), jnp.float32),
            pltpu.VMEM((rows, width), jnp.bfloat16),
            pltpu.VMEM((rows, BLOCK), jnp.bfloat16),
            pltpu.VMEM((4 * rows, width), jnp.bfloat16),
            pltpu.VMEM((8, 128), jnp.float32),
        ],
        in_specs=[hbm, hbm, smem, smem],
        out_specs=[vmem] * 5,
        scratch_shapes=[
            pltpu.VMEM((2, rows, width), jnp.bfloat16),
            pltpu.VMEM((rows, BLOCK), jnp.float32),
            pltpu.SemaphoreType.DMA((2, chunks)),
            pltpu.SemaphoreType.DMA((2, chunks)),
            pltpu.SemaphoreType.DMA((2,)),
            pltpu.SemaphoreType.REGULAR((2,)),
        ],
        compiler_params=pltpu.CompilerParams(
            collective_id=0, has_side_effects=True, vmem_limit_bytes=32 << 20
        ),
        name="exchange",
    )(
        pltpu.with_memory_space_constraint(images, pltpu.HBM),
        pltpu.with_memory_space_constraint(texts, pltpu.HBM),
        logit_scale,
        logit_bias,
    )
    kept = [pltpu.with_memory_space_constraint(x, pltpu.VMEM) for x in kept]
    return pl.pallas_call(
        finish_kernel,
        out_shape=[jax.ShapeDtypeStruct((rows, width), jnp.bfloat16)] * 2,
        in_specs=[vmem] * 5,
        out_specs=[hbm] * 2,
        scratch_shapes=[
            pltpu.VMEM((rows, width), jnp.bfloat16),
            pltpu.SemaphoreType.DMA((1 + rows // BLOCK,)),
        ],
        compiler_params=pltpu.CompilerParams(vmem_limit_bytes=16 << 20),
        name="finish",
    )(*kept)


def solution(mesh):
    placed = (P(("row", "col"), None), P(("row", "col"), None), P(), P())
    return jax.shard_map(
        shards,
        mesh=mesh,
        in_specs=placed,
        out_specs=(P(("row", "col"), None), P(("row", "col"), None)),
        check_vma=False,
    )
```
